256 devices in a mesh: wide: 64 (over z, x_hi, y), narrow: 4 (over x_lo, core).
Axes of the slice: x: 4 (x_hi: 2, x_lo: 2; x = x_hi * 2 + x_lo), y: 4, z: 8, core: 2. Of those that a mesh axis runs over, the one named last changes fastest.
Arguments:
- feats: bfloat16 [131072, 128], P('wide'), may hold values from -6 to 6
- tiles: bfloat16 [16384, 256, 256], P(('wide', 'narrow')), may hold values from 0 to 2, as said below
- tile_rows: int32 [16384], P(('wide', 'narrow')), may hold values from 0 to 511, as said below
- tile_cols: int32 [16384], P(('wide', 'narrow')), may hold values from 0 to 511, as said below
- tile_count: int32 [256], P(('wide', 'narrow')), may hold values from 2 to 64, as said below
- weight: bfloat16 [128, 256], replicated, may hold values from -2 to 2
- cotangent: bfloat16 [131072, 256], P('wide'), may hold values from -6 to 6
Outputs:
- out: bfloat16 [131072, 256], P('wide')
- feats_grad: bfloat16 [131072, 128], P('wide')
- weight_grad: float32 [128, 256], replicated
The draws below stay inside these ranges and needn't reach their ends.
Inputs may be any that keep to these rules, and one draw needn't show every extreme that they name: `tiles`: nonnegative edge weights. `tile_rows`: A slot's row block is one of the 8 row blocks of its device's wide index. `tile_cols`: A slot's column block belongs to a wide index at most 2 away from the slot's own wide index. `tile_count`: some device has all 64 slots live in every draw.
All inputs are finite; a program needn't handle non-finite values.
Results may differ from the reference program's by a relative error of at most 0.019.
Values may be sent and summed in bfloat16 or wider, within the bound.
No kernel may reach another device: no remote copies, remote signals or barrier semaphores. Data moves between devices by JAX's collectives and lax.ppermute only.
A program may use at most 128 MiB of HBM per device.

```python
import jax
import jax.numpy as jnp
from jax import lax

F = 128
H = 256
BLOCK = 256
REACH = 2
ROW_BLOCKS = 8
PAIRS = 64
NODES = 131072
N_WIDE = 64
N_NARROW = 4


def draw_tiles(key, part):
    key = jax.random.fold_in(key, 11)
    key_mask, key_values = jax.random.split(key)
    draw_shape = (N_WIDE * N_NARROW * PAIRS, BLOCK, BLOCK)
    keep_mask = jax.random.uniform(key_mask, draw_shape) < 4.0 / BLOCK
    weights_raw = jax.random.uniform(key_values, draw_shape, minval=0.5, maxval=1.5)
    return jnp.where(keep_mask, weights_raw, 0.0).astype(jnp.bfloat16)


def draw_tile_rows(key, part):
    key = jax.random.fold_in(key, 12)
    slot_index = jnp.arange(N_WIDE * N_NARROW * PAIRS, dtype=jnp.int32)
    wide_index = slot_index // (N_NARROW * PAIRS)
    offsets = jax.random.randint(key, slot_index.shape, 0, ROW_BLOCKS)
    return (wide_index * ROW_BLOCKS + offsets).astype(jnp.int32)


def draw_tile_cols(key, part):
    key = jax.random.fold_in(key, 13)
    key_owner, key_block = jax.random.split(key)
    slot_index = jnp.arange(N_WIDE * N_NARROW * PAIRS, dtype=jnp.int32)
    wide_index = slot_index // (N_NARROW * PAIRS)
    low_owner = jnp.maximum(wide_index - REACH, 0)
    high_owner = jnp.minimum(wide_index + REACH, N_WIDE - 1)
    owner_index = low_owner + jax.random.randint(key_owner, slot_index.shape, 0, high_owner - low_owner + 1)
    inner_slot = slot_index % PAIRS
    owner_index = jnp.where(inner_slot == 0, low_owner, jnp.where(inner_slot == 1, high_owner, owner_index))
    blocks_in = jax.random.randint(key_block, slot_index.shape, 0, ROW_BLOCKS)
    return (owner_index * ROW_BLOCKS + blocks_in).astype(jnp.int32)


def draw_tile_count(key, part):
    key = jax.random.fold_in(key, 14)
    key_first, key_second, key_full = jax.random.split(key, 3)
    devices = N_WIDE * N_NARROW
    first_draw = jax.random.randint(key_first, (devices,), 2, PAIRS + 1)
    second_draw = jax.random.randint(key_second, (devices,), 2, PAIRS + 1)
    full_device = jax.random.randint(key_full, (), 0, devices)
    counts_raw = jnp.minimum(first_draw, second_draw)
    return jnp.where(jnp.arange(devices, dtype=jnp.int32) == full_device, PAIRS, counts_raw).astype(jnp.int32)


def block_scale(stream_key, shape, shards, least, largest):
    def one(axis_at, shards_of):
        draws = jax.random.uniform(jax.random.fold_in(jax.random.fold_in(stream_key, 6), axis_at), (shards_of,), jnp.float32, least / len(shards), largest / len(shards))
        return jnp.repeat(jnp.exp(draws), shape[axis_at] // shards_of).reshape((-1,) + (1,) * (len(shape) - axis_at - 1))

    loudness = one(*shards[0])
    for cut in shards[1:]:
        loudness = loudness * one(*cut)
    return loudness


def bell_draw(rng, extent, width, reach, shards=(), kind=jnp.bfloat16):
    result = width * jax.random.normal(rng, extent, jnp.float32)
    if shards:
        result = result * block_scale(rng, extent, shards, -0.22, 0.18)
    return jnp.clip(result, -reach, reach).astype(kind)


def setup_inputs(seed: int = 0) -> dict:
    arg_keys = jax.random.split(jax.random.key(seed), 8)
    feats = bell_draw(arg_keys[0], (NODES, F), 1.0, 6.0, ((0, 64),))
    tiles = draw_tiles(jax.random.fold_in(arg_keys[7], 71), 0)
    tile_rows = draw_tile_rows(jax.random.fold_in(arg_keys[7], 71), 0)
    tile_cols = draw_tile_cols(jax.random.fold_in(arg_keys[7], 71), 0)
    tile_count = draw_tile_count(jax.random.fold_in(arg_keys[7], 71), 0)
    weight = bell_draw(arg_keys[5], (F, H), (F // 16) ** -0.5, 2.0)
    cotangent = bell_draw(arg_keys[6], (NODES, H), 1.0, 6.0, ((0, 64),))
    return {"feats": feats, "tiles": tiles, "tile_rows": tile_rows, "tile_cols": tile_cols, "tile_count": tile_count, "weight": weight, "cotangent": cotangent}


def reference(feats, tiles, tile_rows, tile_cols, tile_count, weight, cotangent):
    devices = N_WIDE * N_NARROW
    nblocks = ROW_BLOCKS * N_WIDE
    window_span = (2 * REACH + 1) * ROW_BLOCKS
    tiles_dev = tiles.reshape(devices, PAIRS, BLOCK, BLOCK)
    rows_dev = tile_rows.reshape(devices, PAIRS)
    cols_dev = tile_cols.reshape(devices, PAIRS)
    live_mask = (jnp.arange(PAIRS, dtype=jnp.int32)[None, :] < tile_count[:, None]).astype(jnp.float32)
    wide_ids = jnp.arange(devices, dtype=jnp.int32) // N_NARROW

    def add_degree(running, element):
        tile_set, row_ids, live_row = element
        row_sums = lax.optimization_barrier(jnp.sum(tile_set.astype(jnp.float32), axis=2)) * live_row[:, None]
        return (running.at[row_ids].add(row_sums), None)
    degree_blocks, _ = lax.scan(add_degree, jnp.zeros((nblocks, BLOCK), jnp.float32), (tiles_dev, rows_dev, live_mask))
    inv_root = lax.rsqrt(1.0 + degree_blocks.reshape(-1))[:, None]
    scaled = (inv_root * feats.astype(jnp.float32)).astype(jnp.bfloat16)
    scaled_blocks = scaled.reshape(nblocks, BLOCK, F)

    def add_forward(running, element):
        tile_set, row_ids, col_ids, live_row = element
        col_slabs = scaled_blocks[col_ids].astype(jnp.float32)
        products = jnp.einsum('pij,pjf->pif', tile_set.astype(jnp.float32), col_slabs) * live_row[:, None, None]
        return (running.at[row_ids].add(products), None)
    forward_sums, _ = lax.scan(add_forward, jnp.zeros((nblocks, BLOCK, F), jnp.float32), (tiles_dev, rows_dev, cols_dev, live_mask))
    aggregate = (inv_root * (forward_sums.reshape(-1, F) + scaled.astype(jnp.float32))).astype(jnp.bfloat16)
    out = jnp.dot(aggregate, weight, preferred_element_type=jnp.float32).astype(jnp.bfloat16)
    weight_grad = jnp.dot(aggregate.T, cotangent, preferred_element_type=jnp.float32)
    back_rows = jnp.dot(cotangent, weight.T, preferred_element_type=jnp.float32)
    back_scaled = (inv_root * back_rows).astype(jnp.bfloat16)
    back_blocks = back_scaled.reshape(nblocks, BLOCK, F)

    def add_backward(running, element):
        tile_set, row_ids, col_ids, live_row, wide_index = element
        window_base = (jnp.clip(wide_index - REACH, 0, N_WIDE - 2 * REACH - 1) * ROW_BLOCKS).astype(jnp.int32)
        sources = back_blocks[row_ids].astype(jnp.float32)
        products = jnp.einsum('pij,pif->pjf', tile_set.astype(jnp.float32), sources) * live_row[:, None, None]
        local_sums = jnp.zeros((window_span, BLOCK, F), jnp.float32).at[(col_ids - window_base).astype(jnp.int32)].add(products)
        local_sums = lax.optimization_barrier(local_sums.astype(jnp.bfloat16)).astype(jnp.float32)
        current = lax.dynamic_slice_in_dim(running, window_base, window_span, 0)
        return (lax.dynamic_update_slice_in_dim(running, current + local_sums, window_base, 0), None)
    backward_sums, _ = lax.scan(add_backward, jnp.zeros((nblocks, BLOCK, F), jnp.float32), (tiles_dev, rows_dev, cols_dev, live_mask, wide_ids))
    feats_grad = (inv_root * (backward_sums.reshape(-1, F) + back_scaled.astype(jnp.float32))).astype(jnp.bfloat16)
    return (out, feats_grad, weight_grad)
```

```python
import jax
import jax.numpy as jnp
from jax import lax
from jax.experimental import pallas as pl
from jax.experimental.pallas import tpu as pltpu
from jax.sharding import PartitionSpec as P

BLOCK = 256
REACH = 2
STEP = 8
OFFSETS = (-2, -1, 1, 2)
f32 = jnp.float32
bf16 = jnp.bfloat16
VMEM = pl.BlockSpec(memory_space=pltpu.VMEM)
SMEM = pl.BlockSpec(memory_space=pltpu.SMEM)
LIMIT = pltpu.CompilerParams(vmem_limit_bytes=32 * 2**20)

NT = (((1,), (1,)), ((), ()))
TN = (((0,), (0,)), ((), ()))


def shape(dims, dtype):
    return jax.ShapeDtypeStruct(dims, dtype)


def call(kernel, ins, outs, scratch=(), name=None):
    return pl.pallas_call(
        kernel,
        in_specs=ins,
        out_specs=[VMEM] * len(outs),
        out_shape=outs,
        scratch_shapes=list(scratch),
        compiler_params=LIMIT,
        name=name,
    )


def each_step(count, step_fn):
    def body(step, carry):
        step_fn(step * STEP)
        return carry

    lax.fori_loop(0, (count + STEP - 1) // STEP, body, 0)


def turn_kernel(feats_ref, out_ref):
    for block in range(out_ref.shape[0]):
        out_ref[block] = feats_ref[block].T


def degree_kernel(count_ref, rows_ref, tiles_ref, out_ref, total):
    blocks = out_ref.shape[0]
    count = count_ref[0]
    total[...] = jnp.zeros_like(total)
    ones = jnp.ones((8, BLOCK), bf16)

    def step_fn(first):
        sums = [
            lax.dot_general(ones, tiles_ref[first + k], NT, preferred_element_type=f32)
            for k in range(STEP)
        ]
        for k in range(STEP):
            row = jnp.where(first + k < count, rows_ref[first + k], blocks)
            total[row] += sums[k]

    each_step(count, step_fn)
    for block in range(blocks):
        out_ref[block : block + 1] = total[block, 0:1]


def backward_kernel(
    count_ref, rows_ref, slots_ref, tiles_ref, weight_ref, cot_ref, inv_ref,
    back_ref, own_ref, keep_ref, send_ref, total,
):
    blocks = cot_ref.shape[0]
    count = count_ref[0]
    for block in range(blocks):
        rows = lax.dot_general(weight_ref[...], cot_ref[block], NT, preferred_element_type=f32)
        back_ref[block] = (rows * inv_ref[block : block + 1]).astype(bf16)
    total[...] = jnp.zeros_like(total)

    def step_fn(first):
        products = [
            jnp.dot(back_ref[rows_ref[first + k]], tiles_ref[first + k], preferred_element_type=f32)
            for k in range(STEP)
        ]
        for k in range(STEP):
            slot = jnp.where(first + k < count, slots_ref[first + k], 5 * blocks)
            total[slot] += products[k]

    each_step(count, step_fn)
    for part, (ref, at) in enumerate(
        ((own_ref, None), (keep_ref, 0), (send_ref, 0), (keep_ref, 1), (send_ref, 1))
    ):
        for block in range(blocks):
            value = total[part * blocks + block].astype(bf16)
            if at is None:
                ref[block] = value
            else:
                ref[at, block] = value


def forward_kernel(
    place_ref, count_ref, rows_ref, slots_ref, tiles_ref, own_ref, x0, x1, x2, x3, inv_ref, invs_ref,
    keep_ref, send_ref, window, total,
):
    blocks = own_ref.shape[0]
    quarter = own_ref.shape[1] // 4
    count = count_ref[0]
    me = place_ref[0]
    for block in range(blocks):
        window[block] = (own_ref[block].astype(f32) * inv_ref[block : block + 1]).astype(bf16)
    for part, ref in enumerate((x0, x1, x2, x3)):
        who = me ^ part
        for block in range(blocks):
            scale = invs_ref[who, block : block + 1]
            window[(part + 1) * blocks + block] = (ref[block].astype(f32) * scale).astype(bf16)
    total[...] = jnp.zeros_like(total)

    def step_fn(first):
        products = [
            lax.dot_general(
                window[slots_ref[first + k]], tiles_ref[first + k], NT, preferred_element_type=f32
            )
            for k in range(STEP)
        ]
        for k in range(STEP):
            row = jnp.where(first + k < count, rows_ref[first + k], blocks)
            total[row] += products[k]

    each_step(count, step_fn)
    for ref, at, part in ((keep_ref, 0, 0), (send_ref, 0, 1), (keep_ref, 1, 2), (send_ref, 1, 3)):
        start = pl.multiple_of((me ^ part) * quarter, quarter)
        for block in range(blocks):
            ref[at, block] = total[block, pl.ds(start, quarter)].astype(bf16)


def aggregate_kernel(place_ref, mine_ref, other_ref, inv_ref, feats_ref, cot_ref, agg_ref, term_ref):
    blocks = mine_ref.shape[0]
    quarter = mine_ref.shape[1]
    start = pl.multiple_of(place_ref[0] * quarter, quarter)
    term = jnp.zeros(term_ref.shape, f32)
    for block in range(blocks):
        inv = inv_ref[block : block + 1]
        own = (feats_ref[block, pl.ds(start, quarter)].astype(f32) * inv).astype(bf16)
        summed = mine_ref[block].astype(f32) + other_ref[block].astype(f32)
        agg = (inv * (summed + own.astype(f32))).astype(bf16)
        agg_ref[block] = agg
        term = term + jnp.dot(agg, cot_ref[block], preferred_element_type=f32)
    term_ref[...] = term.astype(bf16)


def out_kernel(agg_ref, weight_ref, out_ref):
    parts, blocks, quarter, _ = agg_ref.shape
    for block in range(blocks):
        total = None
        for part in range(parts):
            product = lax.dot_general(
                agg_ref[part, block],
                weight_ref[part * quarter : (part + 1) * quarter],
                TN,
                preferred_element_type=f32,
            )
            total = product if total is None else total + product
        out_ref[block] = total.astype(bf16)


def grad_kernel(place_ref, mine_ref, other_ref, back_ref, inv_ref, out_ref):
    first = place_ref[0] * 2
    for k in range(2):
        inv = inv_ref[pl.ds(first + k, 1)]
        summed = mine_ref[k].astype(f32) + other_ref[k].astype(f32)
        grad = inv * (summed + back_ref[first + k].astype(f32))
        out_ref[k] = grad.T.astype(bf16)


def per_device(feats, tiles, tile_rows, tile_cols, tile_count, weight, cotangent):
    nodes, width = feats.shape
    hidden = cotangent.shape[1]
    blocks = nodes // BLOCK
    quarter = width // 4
    wides = lax.axis_size("wide")
    narrows = lax.axis_size("narrow")
    wide = lax.axis_index("wide")
    me = lax.axis_index("narrow").astype(jnp.int32)
    place = me.reshape(1)

    def swap(x, by):
        return lax.ppermute(x, "narrow", [(i, i ^ by) for i in range(narrows)])

    def fetch(x, sign):
        pairs = [
            (w * narrows + n, (w + sign * OFFSETS[n]) * narrows + n)
            for w in range(wides)
            for n in range(narrows)
            if 0 <= w + sign * OFFSETS[n] < wides
        ]
        return lax.ppermute(x, ("wide", "narrow"), pairs)

    rows = tile_rows - wide * blocks
    offset = tile_cols // blocks - wide
    owner = jnp.where(offset < 0, offset + 2, offset + 1)
    part = jnp.where(offset == 0, 0, 1 + (owner ^ me))
    slots = part * blocks + tile_cols % blocks

    (feats_t,) = call(turn_kernel, [VMEM], [shape((blocks, width, BLOCK), bf16)], name="turn")(
        feats.reshape(blocks, BLOCK, width)
    )
    x0 = fetch(feats_t, -1)

    (degree_part,) = call(
        degree_kernel,
        [SMEM, SMEM, VMEM],
        [shape((blocks, BLOCK), f32)],
        [pltpu.VMEM((blocks + 1, 8, BLOCK), f32)],
        name="degree",
    )(tile_count, rows, tiles)
    degree = 1.0 + jnp.sum(lax.all_gather(degree_part, "narrow"), axis=0)
    inv = lax.rsqrt(degree)
    inv_far = fetch(inv, -1)

    cot = cotangent.reshape(blocks, BLOCK, hidden)
    block_shape = (blocks, width, BLOCK)
    back, q_own, q_keep, q_send = call(
        backward_kernel,
        [SMEM] * 3 + [VMEM] * 4,
        [
            shape(block_shape, bf16),
            shape(block_shape, bf16),
            shape((2,) + block_shape, bf16),
            shape((2,) + block_shape, bf16),
        ],
        [pltpu.VMEM((5 * blocks + 1, width, BLOCK), f32)],
        name="backward",
    )(tile_count, rows, slots, tiles, weight, cot, inv)
    q_half = q_keep.astype(f32) + swap(q_send, 1).astype(f32)
    q_whole = q_half[0] + swap(q_half[1].astype(bf16), 2).astype(f32)
    q_far = fetch(q_whole.astype(bf16), 1)

    x1 = swap(x0, 1)
    x2 = swap(x0, 2)
    x3 = swap(x2, 1)
    invs = lax.all_gather(inv_far, "narrow")
    p_keep, p_send = call(
        forward_kernel,
        [SMEM] * 4 + [VMEM] * 8,
        [shape((2, blocks, quarter, BLOCK), bf16)] * 2,
        [
            pltpu.VMEM((5 * blocks, width, BLOCK), bf16),
            pltpu.VMEM((blocks + 1, width, BLOCK), f32),
        ],
        name="forward",
    )(place, tile_count, rows, slots, tiles, feats_t, x0, x1, x2, x3, inv, invs)
    p_half = p_keep.astype(f32) + swap(p_send, 1).astype(f32)
    p_other = swap(p_half[1].astype(bf16), 2)
    agg, term = call(
        aggregate_kernel,
        [SMEM] + [VMEM] * 5,
        [shape((blocks, quarter, BLOCK), bf16), shape((quarter, hidden), bf16)],
        name="aggregate",
    )(place, p_half[0], p_other, inv, feats_t, cot)

    terms = jnp.broadcast_to(term[None], (wides, quarter, hidden))
    terms = lax.all_to_all(terms, "wide", 0, 0)
    weight_part = jnp.sum(terms.astype(f32), axis=0)
    weight_grad = lax.all_gather(weight_part, "narrow", tiled=True)

    agg_all = lax.all_gather(agg, "narrow")
    (out,) = call(out_kernel, [VMEM] * 2, [shape((blocks, BLOCK, hidden), bf16)], name="out")(
        agg_all, weight
    )

    z = (q_own.astype(f32) + q_far.astype(f32)).reshape(narrows, 2, width, BLOCK)

    def piece(by):
        return lax.dynamic_index_in_dim(z, me ^ by, 0, keepdims=False)

    z_got = swap(jnp.stack([piece(1), piece(3)]).astype(bf16), 1).astype(f32)
    z_mine = piece(0) + z_got[0]
    z_other = swap((piece(2) + z_got[1]).astype(bf16), 2)
    (grad,) = call(
        grad_kernel, [SMEM] + [VMEM] * 4, [shape((2, BLOCK, width), bf16)], name="grad"
    )(place, z_mine, z_other, back, inv)
    feats_grad = lax.all_gather(grad, "narrow", tiled=True)
    return (out.reshape(nodes, hidden), feats_grad.reshape(nodes, width), weight_grad)


def solution(mesh):
    placed = (
        P("wide", None),
        P(("wide", "narrow"), None, None),
        P(("wide", "narrow")),
        P(("wide", "narrow")),
        P(("wide", "narrow")),
        P(),
        P("wide", None),
    )
    return jax.shard_map(
        per_device,
        mesh=mesh,
        in_specs=placed,
        out_specs=(P("wide", None), P("wide", None), P()),
        check_vma=False,
    )
```

```python
import jax
import jax.numpy as jnp
from jax import lax
from jax.experimental import pallas as pl
from jax.experimental.pallas import tpu as pltpu
from jax.sharding import Mesh, PartitionSpec as P

WIDE = ("far", "near")
BLOCK = 256
REACH = 2
STEP = 8
COST = {
    "degree": 10, "scale": 1, "backward": 10, "pass": 1, "forward": 10, "whole": 1,
    "aggregate": 10, "gather": 1, "split": 1, "pack": 1, "grad": 5, "finish": 1, "after": 0,
}
OFFSETS = (-2, -1, 1, 2)
f32 = jnp.float32
bf16 = jnp.bfloat16
VMEM = pl.BlockSpec(memory_space=pltpu.VMEM)
HBM = pl.BlockSpec(memory_space=pltpu.HBM)
SMEM = pl.BlockSpec(memory_space=pltpu.SMEM)

NT = (((1,), (1,)), ((), ()))
TN = (((0,), (0,)), ((), ()))


def shape(dims, dtype):
    return jax.ShapeDtypeStruct(dims, dtype)


def call(kernel, ins, outs, scratch=(), name=None, mib=6):
    return pl.pallas_call(
        kernel,
        in_specs=ins,
        out_specs=[VMEM] * len(outs),
        out_shape=outs,
        scratch_shapes=list(scratch),
        compiler_params=pltpu.CompilerParams(vmem_limit_bytes=mib * 2**20),
        cost_estimate=pl.CostEstimate(
            flops=COST[name] * 10**9, bytes_accessed=COST[name] * 10**6, transcendentals=0
        ),
        name=name,
    )


def each_step(count, step_fn):
    def body(step, carry):
        step_fn(step * STEP)
        return carry

    lax.fori_loop(0, (count + STEP - 1) // STEP, body, 0)


def after(x, *others, first=False):
    def kernel(*refs):
        refs[-1][...] = refs[0][0] if first else refs[0][...]

    (out,) = call(
        kernel, [VMEM] * (1 + len(others)), [shape(x.shape[first:], x.dtype)], name="after"
    )(x, *others)
    return out


def scale_kernel(degrees_ref, feats_ref, inv_ref, out_ref):
    degree = 1.0 + degrees_ref[0]
    for part in range(1, degrees_ref.shape[0]):
        degree = degree + degrees_ref[part]
    inv_ref[...] = lax.rsqrt(degree)
    for block in range(out_ref.shape[0]):
        turned = feats_ref[block].T.astype(f32)
        out_ref[block] = (turned * inv_ref[block : block + 1]).astype(bf16)


def degree_kernel(count_ref, rows_ref, tiles_ref, out_ref, total):
    blocks = out_ref.shape[0]
    count = count_ref[0]
    ones = jnp.ones((8, BLOCK), bf16)

    def prepare():
        total[...] = jnp.zeros_like(total)

    def step_fn(first):
        sums = [
            lax.dot_general(ones, tiles_ref[first + k], NT, preferred_element_type=f32)
            for k in range(STEP)
        ]
        for k in range(STEP):
            row = jnp.where(first + k < count, rows_ref[first + k], blocks)
            total[row] += sums[k]

    prepare()
    each_step(count, step_fn)
    for block in range(blocks):
        out_ref[block : block + 1] = total[block, 0:1]


def backward_kernel(
    count_ref, rows_ref, slots_ref, tiles_ref, weight_ref, cot_ref, inv_ref,
    back_ref, own_ref, keep0_ref, keep2_ref, send1_ref, send3a_ref, send3b_ref, total,
):
    blocks = cot_ref.shape[0]
    count = count_ref[0]

    def prepare():
        for block in range(blocks):
            rows = lax.dot_general(weight_ref[...], cot_ref[block], NT, preferred_element_type=f32)
            back_ref[block] = (rows * inv_ref[block : block + 1]).astype(bf16)
        total[...] = jnp.zeros_like(total)

    def step_fn(first):
        products = [
            jnp.dot(back_ref[rows_ref[first + k]], tiles_ref[first + k], preferred_element_type=f32)
            for k in range(STEP)
        ]
        for k in range(STEP):
            slot = jnp.where(first + k < count, slots_ref[first + k], 5 * blocks)
            total[slot] += products[k]

    prepare()
    each_step(count, step_fn)
    half = blocks // 2
    for part, ref in enumerate((own_ref, keep0_ref, send1_ref, keep2_ref)):
        for block in range(blocks):
            ref[block] = total[part * blocks + block].astype(bf16)
    for block in range(half):
        send3a_ref[block] = total[4 * blocks + block].astype(bf16)
        send3b_ref[block] = total[4 * blocks + half + block].astype(bf16)


def pass_kernel(keep_ref, a_ref, b_ref, out_ref):
    half = a_ref.shape[0]
    for block in range(half):
        got = a_ref[block].astype(f32)
        out_ref[block] = (keep_ref[block].astype(f32) + got).astype(bf16)
        got = b_ref[block].astype(f32)
        out_ref[half + block] = (keep_ref[half + block].astype(f32) + got).astype(bf16)


def forward_kernel(
    place_ref, count_ref, rows_ref, slots_ref, tiles_ref, own_ref, x0, x1, x2, x3, ready_ref,
    keep_ref, send_ref, window, total,
):
    blocks = own_ref.shape[0]
    quarter = own_ref.shape[1] // 4
    count = count_ref[0]
    me = place_ref[0]

    def prepare():
        for part, ref in enumerate((own_ref, x0, x1, x2, x3)):
            for block in range(blocks):
                window[part * blocks + block] = ref[block]
        total[...] = jnp.zeros_like(total)

    def step_fn(first):
        products = [
            lax.dot_general(
                window[slots_ref[first + k]], tiles_ref[first + k], NT, preferred_element_type=f32
            )
            for k in range(STEP)
        ]
        for k in range(STEP):
            row = jnp.where(first + k < count, rows_ref[first + k], blocks)
            total[row] += products[k]

    prepare()
    each_step(count, step_fn)
    for ref, at, part in ((keep_ref, 0, 0), (send_ref, 0, 1), (keep_ref, 1, 2), (send_ref, 1, 3)):
        start = pl.multiple_of((me ^ part) * quarter, quarter)
        for block in range(blocks):
            ref[at, block] = total[block, pl.ds(start, quarter)].astype(bf16)


def whole_kernel(keep_ref, got_ref, other_ref, ready_ref, out_ref):
    for block in range(out_ref.shape[0]):
        whole = keep_ref[block].astype(f32) + got_ref[block].astype(f32)
        out_ref[block] = (whole + other_ref[block].astype(f32)).astype(bf16)


def aggregate_kernel(
    place_ref, mine_ref, got_ref, other_ref, inv_ref, scaled_ref, cot_ref, agg_ref, terms_ref
):
    blocks = other_ref.shape[0]
    quarter = other_ref.shape[1]
    start = pl.multiple_of(place_ref[0] * quarter, quarter)
    term = jnp.zeros(terms_ref.shape[1:], f32)
    for block in range(blocks):
        inv = inv_ref[block : block + 1]
        own = scaled_ref[block, pl.ds(start, quarter)]
        summed = mine_ref[0, block].astype(f32) + got_ref[0, block].astype(f32)
        summed = summed + other_ref[block].astype(f32)
        agg = (inv * (summed + own.astype(f32))).astype(bf16)
        agg_ref[block] = agg
        term = term + jnp.dot(agg, cot_ref[block], preferred_element_type=f32)
    term = term.astype(bf16)
    for part in range(terms_ref.shape[0]):
        terms_ref[part] = term


def gather_kernel(terms_ref, out_ref):
    total = terms_ref[0].astype(f32)
    for part in range(1, terms_ref.shape[0]):
        total = total + terms_ref[part].astype(f32)
    for part in range(out_ref.shape[0]):
        out_ref[part] = total.astype(bf16)


def split_kernel(place_ref, own_ref, far_ref, ready_ref, also_ref, keep_ref, send_ref):
    for ref, at, part in ((keep_ref, 0, 0), (send_ref, 0, 1), (keep_ref, 1, 2), (send_ref, 1, 3)):
        first = (place_ref[0] ^ part) * 2
        for k in range(2):
            total = own_ref[first + k].astype(f32) + far_ref[first + k].astype(f32)
            ref[at, k] = total.astype(bf16)


def grad_kernel(place_ref, keep_ref, got_ref, other_ref, back_ref, inv_ref, out_ref):
    first = place_ref[0] * 2
    for k in range(2):
        inv = inv_ref[pl.ds(first + k, 1)]
        summed = keep_ref[0, k].astype(f32) + got_ref[0, k].astype(f32)
        summed = summed + other_ref[k].astype(f32)
        out_ref[k] = (inv * (summed + back_ref[first + k].astype(f32))).astype(bf16)


def pack_kernel(terms_ref, grad_ref, out_ref):
    quarter = terms_ref.shape[1]
    width = grad_ref.shape[1]
    total = terms_ref[0].astype(f32)
    for part in range(1, terms_ref.shape[0]):
        total = total + terms_ref[part].astype(f32)
    high = total.astype(bf16)
    out_ref[:quarter] = high
    out_ref[quarter : 2 * quarter] = (total - high.astype(f32)).astype(bf16)
    for k in range(2):
        at = 2 * quarter + k * width
        out_ref[at : at + width] = grad_ref[k]


def finish_kernel(
    place_ref, packed_ref, agg0, agg2, agg13, weight_ref, out_ref, grad_ref, weight_grad_ref
):
    parts = packed_ref.shape[0]
    width = weight_ref.shape[0]
    quarter = width // parts
    blocks = out_ref.shape[0] // BLOCK
    for part in range(parts):
        high = packed_ref[part, :quarter].astype(f32)
        low = packed_ref[part, quarter : 2 * quarter].astype(f32)
        weight_grad_ref[part * quarter : (part + 1) * quarter] = high + low
    for block in range(blocks):
        total = None
        for part, agg in enumerate((agg0, agg13.at[0], agg2, agg13.at[1])):
            start = pl.multiple_of((place_ref[0] ^ part) * quarter, quarter)
            product = lax.dot_general(
                agg[block], weight_ref[pl.ds(start, quarter)], TN, preferred_element_type=f32
            )
            total = product if total is None else total + product
        out_ref[block * BLOCK : (block + 1) * BLOCK] = total.astype(bf16)
        part, k = divmod(block, blocks // parts)
        at = 2 * quarter + k * width
        grad_ref[block * BLOCK : (block + 1) * BLOCK] = packed_ref[part, at : at + width].T


def per_device(feats, tiles, tile_rows, tile_cols, tile_count, weight, cotangent):
    nodes, width = feats.shape
    hidden = cotangent.shape[1]
    blocks = nodes // BLOCK
    quarter = width // 4
    wides = lax.axis_size(WIDE)
    nears = lax.axis_size("near")
    fars = lax.axis_size("far")
    narrows = lax.axis_size("narrow")
    wide = lax.axis_index(WIDE)
    me = lax.axis_index("narrow").astype(jnp.int32)
    place = me.reshape(1)

    def swap(x, by):
        return lax.ppermute(x, "narrow", [(i, i ^ by) for i in range(narrows)])

    def fetch(x, sign, turned=0):
        pairs = [
            (w * narrows + n, (w + sign * OFFSETS[n ^ turned]) * narrows + n)
            for w in range(wides)
            for n in range(narrows)
            if 0 <= w + sign * OFFSETS[n ^ turned] < wides
        ]
        return lax.ppermute(x, WIDE + ("narrow",), pairs)

    rows = tile_rows - wide * blocks
    offset = tile_cols // blocks - wide
    owner = jnp.where(offset < 0, offset + 2, offset + 1)
    part = jnp.where(offset == 0, 0, 1 + (owner ^ me))
    slots = part * blocks + tile_cols % blocks

    (degree_part,) = call(
        degree_kernel,
        [SMEM, SMEM, VMEM],
        [shape((blocks, BLOCK), f32)],
        [pltpu.VMEM((blocks + 1, 8, BLOCK), f32)],
        name="degree",
        mib=4,
    )(tile_count, rows, tiles)
    block_shape = (blocks, width, BLOCK)
    inv, scaled = call(
        scale_kernel,
        [VMEM] * 2,
        [shape((blocks, BLOCK), f32), shape(block_shape, bf16)],
        name="scale",
    )(lax.all_gather(degree_part, "narrow"), feats.reshape(blocks, BLOCK, width))
    x0 = fetch(scaled, -1)
    x2 = fetch(scaled, -1, 2)

    cot = cotangent.reshape(blocks, BLOCK, hidden)
    half_shape = (blocks // 2, width, BLOCK)
    back, q_own, q_keep0, q_keep2, q_send1, q_send3a, q_send3b = call(
        backward_kernel,
        [SMEM] * 3 + [VMEM] * 4,
        [shape(block_shape, bf16)] * 5 + [shape(half_shape, bf16)] * 2,
        [pltpu.VMEM((5 * blocks + 1, width, BLOCK), f32)],
        name="backward",
        mib=12,
    )(tile_count, rows, slots, tiles, weight, cot, inv)
    (q_pass,) = call(pass_kernel, [VMEM] * 3, [shape(block_shape, bf16)], name="pass")(
        q_keep2, swap(q_send3a, 1), swap(q_send3b, 1)
    )
    q_got = swap(q_send1, 1)
    q_other = swap(q_pass, 2)

    x1 = swap(after(x0, q_pass), 1)
    x3 = swap(after(x2, q_pass), 1)
    p_keep, p_send = call(
        forward_kernel,
        [SMEM] * 4 + [VMEM] * 6 + [HBM],
        [shape((2, blocks, quarter, BLOCK), bf16)] * 2,
        [
            pltpu.VMEM((5 * blocks, width, BLOCK), bf16),
            pltpu.VMEM((blocks + 1, width, BLOCK), f32),
        ],
        name="forward",
        mib=12,
    )(place, tile_count, rows, slots, tiles, scaled, x0, x1, x2, x3, q_other)
    p_got = swap(p_send, 1)
    p_pass = (p_keep[1].astype(f32) + p_got[1].astype(f32)).astype(bf16)
    p_other = swap(p_pass, 2)
    (q_whole,) = call(whole_kernel, [VMEM] * 3 + [HBM], [shape(block_shape, bf16)], name="whole")(
        q_keep0, q_got, q_other, p_pass
    )
    q_far = fetch(q_whole, 1)
    agg, terms = call(
        aggregate_kernel,
        [SMEM] + [VMEM] * 6,
        [
            shape((blocks, quarter, BLOCK), bf16),
            shape((fars, quarter, hidden), bf16),
        ],
        name="aggregate",
    )(place, p_keep, p_got, p_other, inv, scaled, cot)
    terms = lax.all_to_all(terms, "far", 0, 0)
    agg2 = swap(agg, 2)
    agg13 = swap(jnp.stack([agg, agg2]), 1)
    (terms,) = call(
        gather_kernel, [VMEM], [shape((nears, quarter, hidden), bf16)], name="gather"
    )(terms)

    z_keep, z_send = call(
        split_kernel,
        [SMEM] + [VMEM] * 2 + [HBM] * 2,
        [shape((2, 2, width, BLOCK), bf16)] * 2,
        name="split",
    )(place, q_own, q_far, terms, agg2)
    z_got = swap(z_send, 1)
    z_pass = (z_keep[1].astype(f32) + z_got[1].astype(f32)).astype(bf16)
    z_other = swap(z_pass, 2)
    terms = lax.all_to_all(after(terms, z_pass), "near", 0, 0)
    (grad,) = call(
        grad_kernel, [SMEM] + [VMEM] * 5, [shape((2, width, BLOCK), bf16)], name="grad"
    )(place, z_keep, z_got, z_other, back, inv)
    (packed,) = call(
        pack_kernel,
        [VMEM] * 2,
        [shape((2 * quarter + 2 * width, BLOCK), bf16)],
        name="pack",
    )(terms, grad)
    packed = lax.all_gather(packed, "narrow")
    out, feats_grad, weight_grad = call(
        finish_kernel,
        [SMEM] + [VMEM] * 5,
        [
            shape((nodes, hidden), bf16),
            shape((nodes, width), bf16),
            shape((width, hidden), f32),
        ],
        name="finish",
    )(place, packed, agg, agg2, agg13, weight)
    return (out, feats_grad, weight_grad)


def solution(mesh):
    mesh = Mesh(mesh.devices.reshape(8, 8, 4), ("far", "near", "narrow"))
    rows = P(WIDE, None)
    slots = P(WIDE + ("narrow",))
    placed = (rows, P(WIDE + ("narrow",), None, None), slots, slots, slots, P(), rows)
    return jax.shard_map(
        per_device,
        mesh=mesh,
        in_specs=placed,
        out_specs=(rows, rows, P()),
        check_vma=False,
    )
```

```python
import jax
import jax.numpy as jnp
from jax import lax
from jax.experimental import pallas as pl
from jax.experimental.pallas import tpu as pltpu
from jax.sharding import Mesh, PartitionSpec as P

WIDE = ("far", "near")
BLOCK = 256
REACH = 2
STEP = 8
COST = {
    "degree": 10, "scale": 1, "backward": 10, "pass": 1, "forward": 10, "whole": 1,
    "aggregate": 10, "gather": 1, "add": 1, "finish": 10, "weight_grad": 1, "after": 0,
}
OFFSETS = (-1, 1, 2, -2)
f32 = jnp.float32
bf16 = jnp.bfloat16
VMEM = pl.BlockSpec(memory_space=pltpu.VMEM)
HBM = pl.BlockSpec(memory_space=pltpu.HBM)
SMEM = pl.BlockSpec(memory_space=pltpu.SMEM)

NT = (((1,), (1,)), ((), ()))
TN = (((0,), (0,)), ((), ()))


def shape(dims, dtype):
    return jax.ShapeDtypeStruct(dims, dtype)


def call(kernel, ins, outs, scratch=(), name=None, mib=6):
    return pl.pallas_call(
        kernel,
        in_specs=ins,
        out_specs=[VMEM] * len(outs),
        out_shape=outs,
        scratch_shapes=list(scratch),
        compiler_params=pltpu.CompilerParams(vmem_limit_bytes=mib * 2**20),
        cost_estimate=pl.CostEstimate(
            flops=COST[name] * 10**9, bytes_accessed=COST[name] * 10**6, transcendentals=0
        ),
        name=name,
    )


def each_step(count, step_fn):
    def body(step, carry):
        step_fn(step * STEP)
        return carry

    lax.fori_loop(0, (count + STEP - 1) // STEP, body, 0)


def after(x, *others, first=False):
    def kernel(*refs):
        refs[-1][...] = refs[0][0] if first else refs[0][...]

    (out,) = call(
        kernel, [VMEM] * (1 + len(others)), [shape(x.shape[first:], x.dtype)], name="after"
    )(x, *others)
    return out


def scale_kernel(degrees_ref, feats_ref, inv_ref, out_ref):
    degree = 1.0 + degrees_ref[0]
    for part in range(1, degrees_ref.shape[0]):
        degree = degree + degrees_ref[part]
    inv_ref[...] = lax.rsqrt(degree)
    for block in range(out_ref.shape[0]):
        turned = feats_ref[block].T.astype(f32)
        out_ref[block] = (turned * inv_ref[block : block + 1]).astype(bf16)


def degree_kernel(count_ref, rows_ref, tiles_ref, out_ref, total):
    blocks = out_ref.shape[0]
    count = count_ref[0]
    ones = jnp.ones((8, BLOCK), bf16)

    def prepare():
        total[...] = jnp.zeros_like(total)

    def step_fn(first):
        sums = [
            lax.dot_general(ones, tiles_ref[first + k], NT, preferred_element_type=f32)
            for k in range(STEP)
        ]
        for k in range(STEP):
            row = jnp.where(first + k < count, rows_ref[first + k], blocks)
            total[row] += sums[k]

    prepare()
    each_step(count, step_fn)
    for block in range(blocks):
        out_ref[block : block + 1] = total[block, 0:1]


def backward_kernel(
    count_ref, rows_ref, slots_ref, tiles_ref, weight_ref, cot_ref, inv_ref,
    back_ref, own_ref, keep0_ref, keep2_ref, send1_ref, send3a_ref, send3b_ref, total,
):
    blocks = cot_ref.shape[0]
    count = count_ref[0]

    def prepare():
        for block in range(blocks):
            rows = lax.dot_general(weight_ref[...], cot_ref[block], NT, preferred_element_type=f32)
            back_ref[block] = (rows * inv_ref[block : block + 1]).astype(bf16)
        total[...] = jnp.zeros_like(total)

    def step_fn(first):
        products = [
            jnp.dot(back_ref[rows_ref[first + k]], tiles_ref[first + k], preferred_element_type=f32)
            for k in range(STEP)
        ]
        for k in range(STEP):
            slot = jnp.where(first + k < count, slots_ref[first + k], 5 * blocks)
            total[slot] += products[k]

    prepare()
    each_step(count, step_fn)
    half = blocks // 2
    for part, ref in enumerate((own_ref, keep0_ref, send1_ref, keep2_ref)):
        for block in range(blocks):
            ref[block] = total[part * blocks + block].astype(bf16)
    for block in range(half):
        send3a_ref[block] = total[4 * blocks + block].astype(bf16)
        send3b_ref[block] = total[4 * blocks + half + block].astype(bf16)


def pass_kernel(keep_ref, a_ref, b_ref, out_ref):
    half = a_ref.shape[0]
    for block in range(half):
        got = a_ref[block].astype(f32)
        out_ref[block] = (keep_ref[block].astype(f32) + got).astype(bf16)
        got = b_ref[block].astype(f32)
        out_ref[half + block] = (keep_ref[half + block].astype(f32) + got).astype(bf16)


def forward_kernel(
    place_ref, count_ref, rows_ref, slots_ref, tiles_ref, own_ref, x0, x1, x2, x3, ready_ref,
    keep_ref, send_ref, window, total,
):
    blocks = own_ref.shape[0]
    quarter = own_ref.shape[1] // 4
    count = count_ref[0]
    me = place_ref[0]

    def prepare():
        for part, ref in enumerate((own_ref, x0, x1, x2, x3)):
            for block in range(blocks):
                window[part * blocks + block] = ref[block]
        total[...] = jnp.zeros_like(total)

    def step_fn(first):
        products = [
            lax.dot_general(
                window[slots_ref[first + k]], tiles_ref[first + k], NT, preferred_element_type=f32
            )
            for k in range(STEP)
        ]
        for k in range(STEP):
            row = jnp.where(first + k < count, rows_ref[first + k], blocks)
            total[row] += products[k]

    prepare()
    each_step(count, step_fn)
    for ref, at, part in ((keep_ref, 0, 0), (send_ref, 0, 1), (keep_ref, 1, 2), (send_ref, 1, 3)):
        start = pl.multiple_of((me ^ part) * quarter, quarter)
        for block in range(blocks):
            ref[at, block] = total[block, pl.ds(start, quarter)].astype(bf16)


def whole_kernel(keep_ref, got_ref, other_ref, ready_ref, out_ref):
    for block in range(out_ref.shape[0]):
        whole = keep_ref[block].astype(f32) + got_ref[block].astype(f32)
        out_ref[block] = (whole + other_ref[block].astype(f32)).astype(bf16)


def aggregate_kernel(
    place_ref, mine_ref, got_ref, other_ref, inv_ref, scaled_ref, cot_ref, agg_ref, terms_ref
):
    blocks = other_ref.shape[0]
    quarter = other_ref.shape[1]
    start = pl.multiple_of(place_ref[0] * quarter, quarter)
    term = jnp.zeros(terms_ref.shape[1:], f32)
    for block in range(blocks):
        inv = inv_ref[block : block + 1]
        own = scaled_ref[block, pl.ds(start, quarter)]
        summed = mine_ref[0, block].astype(f32) + got_ref[0, block].astype(f32)
        summed = summed + other_ref[block].astype(f32)
        agg = (inv * (summed + own.astype(f32))).astype(bf16)
        agg_ref[block] = agg
        term = term + jnp.dot(agg, cot_ref[block], preferred_element_type=f32)
    term = term.astype(bf16)
    for part in range(terms_ref.shape[0]):
        terms_ref[part] = term


def gather_kernel(terms_ref, out_ref):
    total = terms_ref[0].astype(f32)
    for part in range(1, terms_ref.shape[0]):
        total = total + terms_ref[part].astype(f32)
    for part in range(out_ref.shape[0]):
        out_ref[part] = total.astype(bf16)


def add_kernel(a_ref, b_ref, *refs):
    for block in range(a_ref.shape[0]):
        refs[-1][block] = (a_ref[block].astype(f32) + b_ref[block].astype(f32)).astype(bf16)


def finish_kernel(
    place_ref, agg0, agg2, agg13, weight_ref, pair_ref, other_ref, back_ref, inv_ref,
    out_ref, grad_ref,
):
    blocks, quarter, _ = agg0.shape
    for block in range(blocks):
        rows = slice(block * BLOCK, (block + 1) * BLOCK)
        total = None
        for part, agg in enumerate((agg0, agg13.at[0], agg2, agg13.at[1])):
            start = pl.multiple_of((place_ref[0] ^ part) * quarter, quarter)
            product = lax.dot_general(
                agg[block], weight_ref[pl.ds(start, quarter)], TN, preferred_element_type=f32
            )
            total = product if total is None else total + product
        out_ref[rows] = total.astype(bf16)
        summed = pair_ref[block].astype(f32) + other_ref[block].astype(f32)
        grad = inv_ref[block : block + 1] * (summed + back_ref[block].astype(f32))
        grad_ref[rows] = grad.astype(bf16).T


def weight_grad_kernel(terms_ref, ready_ref, out_ref):
    quarter = terms_ref.shape[1]
    parts = out_ref.shape[0] // quarter
    for part in range(parts):
        total = terms_ref[part].astype(f32)
        for at in range(part + parts, terms_ref.shape[0], parts):
            total = total + terms_ref[at].astype(f32)
        out_ref[part * quarter : (part + 1) * quarter] = total


def per_device(feats, tiles, tile_rows, tile_cols, tile_count, weight, cotangent):
    nodes, width = feats.shape
    hidden = cotangent.shape[1]
    blocks = nodes // BLOCK
    quarter = width // 4
    wides = lax.axis_size(WIDE)
    nears = lax.axis_size("near")
    fars = lax.axis_size("far")
    narrows = lax.axis_size("narrow")
    wide = lax.axis_index(WIDE)
    me = lax.axis_index("narrow").astype(jnp.int32)
    place = me.reshape(1)

    def swap(x, by):
        return lax.ppermute(x, "narrow", [(i, i ^ by) for i in range(narrows)])

    def fetch(x, sign, turned=0):
        pairs = [
            (w * narrows + n, (w + sign * OFFSETS[n ^ turned]) * narrows + n)
            for w in range(wides)
            for n in range(narrows)
            if 0 <= w + sign * OFFSETS[n ^ turned] < wides
        ]
        return lax.ppermute(x, WIDE + ("narrow",), pairs)

    rows = tile_rows - wide * blocks
    offset = tile_cols // blocks - wide
    owner = sum(jnp.where(offset == OFFSETS[n], n, 0) for n in range(narrows))
    part = jnp.where(offset == 0, 0, 1 + (owner ^ me))
    slots = part * blocks + tile_cols % blocks

    (degree_part,) = call(
        degree_kernel,
        [SMEM, SMEM, VMEM],
        [shape((blocks, BLOCK), f32)],
        [pltpu.VMEM((blocks + 1, 8, BLOCK), f32)],
        name="degree",
        mib=4,
    )(tile_count, rows, tiles)
    block_shape = (blocks, width, BLOCK)
    inv, scaled = call(
        scale_kernel,
        [VMEM] * 2,
        [shape((blocks, BLOCK), f32), shape(block_shape, bf16)],
        name="scale",
    )(lax.all_gather(degree_part, "narrow"), feats.reshape(blocks, BLOCK, width))
    x0 = fetch(scaled, -1)
    x2 = fetch(scaled, -1, 2)

    cot = cotangent.reshape(blocks, BLOCK, hidden)
    half_shape = (blocks // 2, width, BLOCK)
    back, q_own, q_keep0, q_keep2, q_send1, q_send3a, q_send3b = call(
        backward_kernel,
        [SMEM] * 3 + [VMEM] * 4,
        [shape(block_shape, bf16)] * 5 + [shape(half_shape, bf16)] * 2,
        [pltpu.VMEM((5 * blocks + 1, width, BLOCK), f32)],
        name="backward",
        mib=12,
    )(tile_count, rows, slots, tiles, weight, cot, inv)
    (q_pass,) = call(pass_kernel, [VMEM] * 3, [shape(block_shape, bf16)], name="pass")(
        q_keep2, swap(q_send3a, 1), swap(q_send3b, 1)
    )
    q_got = swap(q_send1, 1)
    q_other = swap(q_pass, 2)

    x1 = swap(after(x0, q_pass), 1)
    x3 = swap(after(x2, q_pass), 1)
    p_keep, p_send = call(
        forward_kernel,
        [SMEM] * 4 + [VMEM] * 6 + [HBM],
        [shape((2, blocks, quarter, BLOCK), bf16)] * 2,
        [
            pltpu.VMEM((5 * blocks, width, BLOCK), bf16),
            pltpu.VMEM((blocks + 1, width, BLOCK), f32),
        ],
        name="forward",
        mib=12,
    )(place, tile_count, rows, slots, tiles, scaled, x0, x1, x2, x3, q_other)
    p_got = swap(p_send, 1)
    p_pass = (p_keep[1].astype(f32) + p_got[1].astype(f32)).astype(bf16)
    p_other = swap(p_pass, 2)
    (q_whole,) = call(whole_kernel, [VMEM] * 3 + [HBM], [shape(block_shape, bf16)], name="whole")(
        q_keep0, q_got, q_other, p_pass
    )
    q_far = fetch(q_whole, 1)
    agg, terms = call(
        aggregate_kernel,
        [SMEM] + [VMEM] * 6,
        [
            shape((blocks, quarter, BLOCK), bf16),
            shape((fars, quarter, hidden), bf16),
        ],
        name="aggregate",
    )(place, p_keep, p_got, p_other, inv, scaled, cot)
    terms = lax.all_to_all(terms, "far", 0, 0)
    agg2 = swap(agg, 2)
    agg13 = swap(jnp.stack([agg, agg2]), 1)
    (terms,) = call(
        gather_kernel, [VMEM], [shape((nears * narrows, quarter, hidden), bf16)], name="gather"
    )(terms)

    (z,) = call(
        add_kernel, [VMEM] * 2 + [HBM] * 2, [shape(block_shape, bf16)], name="add"
    )(q_own, q_far, terms, agg2)
    (z_pair,) = call(add_kernel, [VMEM] * 2, [shape(block_shape, bf16)], name="add")(z, swap(z, 1))
    z_other = swap(z_pair, 2)
    terms = lax.all_to_all(after(terms, z_pair), ("near", "narrow"), 0, 0)
    out, feats_grad = call(
        finish_kernel,
        [SMEM] + [VMEM] * 8,
        [shape((nodes, hidden), bf16), shape((nodes, width), bf16)],
        name="finish",
    )(place, agg, agg2, agg13, weight, z_pair, z_other, back, inv)
    (weight_grad,) = call(
        weight_grad_kernel, [VMEM, HBM], [shape((width, hidden), f32)], name="weight_grad"
    )(terms, out)
    return (out, feats_grad, weight_grad)


def solution(mesh):
    mesh = Mesh(mesh.devices.reshape(8, 8, 4), ("far", "near", "narrow"))
    rows = P(WIDE, None)
    slots = P(WIDE + ("narrow",))
    placed = (rows, P(WIDE + ("narrow",), None, None), slots, slots, slots, P(), rows)
    return jax.shard_map(
        per_device,
        mesh=mesh,
        in_specs=placed,
        out_specs=(rows, rows, P()),
        check_vma=False,
    )
```

```python
import jax
import jax.numpy as jnp
from jax import lax
from jax.experimental import pallas as pl
from jax.experimental.pallas import tpu as pltpu
from jax.sharding import Mesh, PartitionSpec as P

WIDE = ("far", "near")
BLOCK = 256
REACH = 2
STEP = 16
COST = {
    "degree": 10, "scale": 1, "backward": 10, "pass": 1, "forward": 10, "whole": 1,
    "aggregate": 10, "gather": 1, "add": 1, "finish": 10, "weight_grad": 1, "after": 0,
}
OFFSETS = (-1, 1, 2, -2)
f32 = jnp.float32
bf16 = jnp.bfloat16
VMEM = pl.BlockSpec(memory_space=pltpu.VMEM)
HBM = pl.BlockSpec(memory_space=pltpu.HBM)
SMEM = pl.BlockSpec(memory_space=pltpu.SMEM)

NT = (((1,), (1,)), ((), ()))
TN = (((0,), (0,)), ((), ()))


def shape(dims, dtype):
    return jax.ShapeDtypeStruct(dims, dtype)


def call(kernel, ins, outs, scratch=(), name=None, mib=6):
    return pl.pallas_call(
        kernel,
        in_specs=ins,
        out_specs=[VMEM] * len(outs),
        out_shape=outs,
        scratch_shapes=list(scratch),
        compiler_params=pltpu.CompilerParams(vmem_limit_bytes=mib * 2**20),
        cost_estimate=pl.CostEstimate(
            flops=COST[name] * 10**9, bytes_accessed=COST[name] * 10**6, transcendentals=0
        ),
        name=name,
    )


def each_step(count, step_fn):
    def body(step, carry):
        step_fn(step * STEP)
        return carry

    lax.fori_loop(0, (count + STEP - 1) // STEP, body, 0)


def after(x, *others, first=False):
    def kernel(*refs):
        refs[-1][...] = refs[0][0] if first else refs[0][...]

    (out,) = call(
        kernel, [VMEM] * (1 + len(others)), [shape(x.shape[first:], x.dtype)], name="after"
    )(x, *others)
    return out


def scale_kernel(degrees_ref, feats_ref, inv_ref, out_ref):
    degree = 1.0 + degrees_ref[0]
    for part in range(1, degrees_ref.shape[0]):
        degree = degree + degrees_ref[part]
    inv_ref[...] = lax.rsqrt(degree)
    for block in range(out_ref.shape[0]):
        turned = feats_ref[block].T.astype(f32)
        out_ref[block] = (turned * inv_ref[block : block + 1]).astype(bf16)


def degree_kernel(count_ref, rows_ref, tiles_ref, out_ref, total):
    blocks = out_ref.shape[0]
    count = count_ref[0]
    ones = jnp.ones((8, BLOCK), bf16)

    def prepare():
        total[...] = jnp.zeros_like(total)

    def step_fn(first):
        sums = [
            lax.dot_general(ones, tiles_ref[first + k], NT, preferred_element_type=f32)
            for k in range(STEP)
        ]
        for k in range(STEP):
            row = jnp.where(first + k < count, rows_ref[first + k], blocks)
            total[row] += sums[k]

    prepare()
    each_step(count, step_fn)
    for block in range(blocks):
        out_ref[block : block + 1] = total[block, 0:1]


def backward_kernel(
    count_ref, rows_ref, slots_ref, tiles_ref, weight_ref, cot_ref, inv_ref,
    back_ref, own_ref, keep0_ref, keep2_ref, send1_ref, send3a_ref, send3b_ref, total,
):
    blocks = cot_ref.shape[0]
    count = count_ref[0]

    def prepare():
        for block in range(blocks):
            rows = lax.dot_general(weight_ref[...], cot_ref[block], NT, preferred_element_type=f32)
            back_ref[block] = (rows * inv_ref[block : block + 1]).astype(bf16)
        total[...] = jnp.zeros_like(total)

    def step_fn(first):
        products = [
            jnp.dot(back_ref[rows_ref[first + k]], tiles_ref[first + k], preferred_element_type=f32)
            for k in range(STEP)
        ]
        for k in range(STEP):
            slot = jnp.where(first + k < count, slots_ref[first + k], 5 * blocks)
            total[slot] += products[k]

    prepare()
    each_step(count, step_fn)
    half = blocks // 2
    for part, ref in enumerate((own_ref, keep0_ref, send1_ref, keep2_ref)):
        for block in range(blocks):
            ref[block] = total[part * blocks + block].astype(bf16)
    for block in range(half):
        send3a_ref[block] = total[4 * blocks + block].astype(bf16)
        send3b_ref[block] = total[4 * blocks + half + block].astype(bf16)


def pass_kernel(keep_ref, a_ref, b_ref, out_ref):
    half = a_ref.shape[0]
    for block in range(half):
        got = a_ref[block].astype(f32)
        out_ref[block] = (keep_ref[block].astype(f32) + got).astype(bf16)
        got = b_ref[block].astype(f32)
        out_ref[half + block] = (keep_ref[half + block].astype(f32) + got).astype(bf16)


def forward_kernel(
    place_ref, count_ref, rows_ref, slots_ref, tiles_ref, own_ref, x0, x1, x2, x3, ready_ref,
    keep_ref, send_ref, window, total,
):
    blocks = own_ref.shape[0]
    quarter = own_ref.shape[1] // 4
    count = count_ref[0]
    me = place_ref[0]

    def prepare():
        for part, ref in enumerate((own_ref, x0, x1, x2, x3)):
            for block in range(blocks):
                window[part * blocks + block] = ref[block]
        total[...] = jnp.zeros_like(total)

    def step_fn(first):
        products = [
            lax.dot_general(
                window[slots_ref[first + k]], tiles_ref[first + k], NT, preferred_element_type=f32
            )
            for k in range(STEP)
        ]
        for k in range(STEP):
            row = jnp.where(first + k < count, rows_ref[first + k], blocks)
            total[row] += products[k]

    prepare()
    each_step(count, step_fn)
    for ref, at, part in ((keep_ref, 0, 0), (send_ref, 0, 1), (keep_ref, 1, 2), (send_ref, 1, 3)):
        start = pl.multiple_of((me ^ part) * quarter, quarter)
        for block in range(blocks):
            ref[at, block] = total[block, pl.ds(start, quarter)].astype(bf16)


def whole_kernel(keep_ref, got_ref, other_ref, ready_ref, out_ref):
    for block in range(out_ref.shape[0]):
        whole = keep_ref[block].astype(f32) + got_ref[block].astype(f32)
        out_ref[block] = (whole + other_ref[block].astype(f32)).astype(bf16)


def aggregate_kernel(
    place_ref, mine_ref, got_ref, other_ref, inv_ref, scaled_ref, cot_ref, agg_ref, terms_ref
):
    blocks = other_ref.shape[0]
    quarter = other_ref.shape[1]
    start = pl.multiple_of(place_ref[0] * quarter, quarter)
    term = jnp.zeros(terms_ref.shape[1:], f32)
    for block in range(blocks):
        inv = inv_ref[block : block + 1]
        own = scaled_ref[block, pl.ds(start, quarter)]
        summed = mine_ref[0, block].astype(f32) + got_ref[0, block].astype(f32)
        summed = summed + other_ref[block].astype(f32)
        agg = (inv * (summed + own.astype(f32))).astype(bf16)
        agg_ref[block] = agg
        term = term + jnp.dot(agg, cot_ref[block], preferred_element_type=f32)
    term = term.astype(bf16)
    for part in range(terms_ref.shape[0]):
        terms_ref[part] = term


def gather_kernel(terms_ref, out_ref):
    total = terms_ref[0].astype(f32)
    for part in range(1, terms_ref.shape[0]):
        total = total + terms_ref[part].astype(f32)
    for part in range(out_ref.shape[0]):
        out_ref[part] = total.astype(bf16)


def add_kernel(a_ref, b_ref, *refs):
    for block in range(a_ref.shape[0]):
        refs[-1][block] = (a_ref[block].astype(f32) + b_ref[block].astype(f32)).astype(bf16)


def finish_kernel(
    place_ref, agg0, agg2, agg13, weight_ref, pair_ref, other_ref, back_ref, inv_ref,
    out_ref, grad_ref,
):
    blocks, quarter, _ = agg0.shape
    for block in range(blocks):
        rows = slice(block * BLOCK, (block + 1) * BLOCK)
        total = None
        for part, agg in enumerate((agg0, agg13.at[0], agg2, agg13.at[1])):
            start = pl.multiple_of((place_ref[0] ^ part) * quarter, quarter)
            product = lax.dot_general(
                agg[block], weight_ref[pl.ds(start, quarter)], TN, preferred_element_type=f32
            )
            total = product if total is None else total + product
        out_ref[rows] = total.astype(bf16)
        summed = pair_ref[block].astype(f32) + other_ref[block].astype(f32)
        grad = inv_ref[block : block + 1] * (summed + back_ref[block].astype(f32))
        grad_ref[rows] = grad.astype(bf16).T


def weight_grad_kernel(terms_ref, ready_ref, out_ref):
    quarter = terms_ref.shape[1]
    parts = out_ref.shape[0] // quarter
    for part in range(parts):
        total = terms_ref[part].astype(f32)
        for at in range(part + parts, terms_ref.shape[0], parts):
            total = total + terms_ref[at].astype(f32)
        out_ref[part * quarter : (part + 1) * quarter] = total


def per_device(feats, tiles, tile_rows, tile_cols, tile_count, weight, cotangent):
    nodes, width = feats.shape
    hidden = cotangent.shape[1]
    blocks = nodes // BLOCK
    quarter = width // 4
    wides = lax.axis_size(WIDE)
    nears = lax.axis_size("near")
    fars = lax.axis_size("far")
    narrows = lax.axis_size("narrow")
    wide = lax.axis_index(WIDE)
    me = lax.axis_index("narrow").astype(jnp.int32)
    place = me.reshape(1)

    def swap(x, by):
        return lax.ppermute(x, "narrow", [(i, i ^ by) for i in range(narrows)])

    def fetch(x, sign, turned=0):
        pairs = [
            (w * narrows + n, (w + sign * OFFSETS[n ^ turned]) * narrows + n)
            for w in range(wides)
            for n in range(narrows)
            if 0 <= w + sign * OFFSETS[n ^ turned] < wides
        ]
        return lax.ppermute(x, WIDE + ("narrow",), pairs)

    rows = tile_rows - wide * blocks
    offset = tile_cols // blocks - wide
    owner = sum(jnp.where(offset == OFFSETS[n], n, 0) for n in range(narrows))
    part = jnp.where(offset == 0, 0, 1 + (owner ^ me))
    slots = part * blocks + tile_cols % blocks

    (degree_part,) = call(
        degree_kernel,
        [SMEM, SMEM, VMEM],
        [shape((blocks, BLOCK), f32)],
        [pltpu.VMEM((blocks + 1, 8, BLOCK), f32)],
        name="degree",
        mib=4,
    )(tile_count, rows, tiles)
    block_shape = (blocks, width, BLOCK)
    inv, scaled = call(
        scale_kernel,
        [VMEM] * 2,
        [shape((blocks, BLOCK), f32), shape(block_shape, bf16)],
        name="scale",
    )(lax.all_gather(degree_part, "narrow"), feats.reshape(blocks, BLOCK, width))
    x0 = fetch(scaled, -1)
    x2 = fetch(scaled, -1, 2)

    cot = cotangent.reshape(blocks, BLOCK, hidden)
    half_shape = (blocks // 2, width, BLOCK)
    back, q_own, q_keep0, q_keep2, q_send1, q_send3a, q_send3b = call(
        backward_kernel,
        [SMEM] * 3 + [VMEM] * 4,
        [shape(block_shape, bf16)] * 5 + [shape(half_shape, bf16)] * 2,
        [pltpu.VMEM((5 * blocks + 1, width, BLOCK), f32)],
        name="backward",
        mib=12,
    )(tile_count, rows, slots, tiles, weight, cot, inv)
    (q_pass,) = call(pass_kernel, [VMEM] * 3, [shape(block_shape, bf16)], name="pass")(
        q_keep2, swap(q_send3a, 1), swap(q_send3b, 1)
    )
    q_got = swap(q_send1, 1)
    q_other = swap(q_pass, 2)

    x1 = swap(after(x0, q_pass), 1)
    x3 = swap(after(x2, q_pass), 1)
    p_keep, p_send = call(
        forward_kernel,
        [SMEM] * 4 + [VMEM] * 6 + [HBM],
        [shape((2, blocks, quarter, BLOCK), bf16)] * 2,
        [
            pltpu.VMEM((5 * blocks, width, BLOCK), bf16),
            pltpu.VMEM((blocks + 1, width, BLOCK), f32),
        ],
        name="forward",
        mib=12,
    )(place, tile_count, rows, slots, tiles, scaled, x0, x1, x2, x3, q_other)
    p_got = swap(p_send, 1)
    p_pass = (p_keep[1].astype(f32) + p_got[1].astype(f32)).astype(bf16)
    p_other = swap(p_pass, 2)
    (q_whole,) = call(whole_kernel, [VMEM] * 3 + [HBM], [shape(block_shape, bf16)], name="whole")(
        q_keep0, q_got, q_other, p_pass
    )
    q_far = fetch(q_whole, 1)
    agg, terms = call(
        aggregate_kernel,
        [SMEM] + [VMEM] * 6,
        [
            shape((blocks, quarter, BLOCK), bf16),
            shape((fars, quarter, hidden), bf16),
        ],
        name="aggregate",
    )(place, p_keep, p_got, p_other, inv, scaled, cot)
    terms = lax.all_to_all(terms, "far", 0, 0)
    agg2 = swap(agg, 2)
    agg13 = swap(jnp.stack([agg, agg2]), 1)
    (terms,) = call(
        gather_kernel, [VMEM], [shape((nears * narrows, quarter, hidden), bf16)], name="gather"
    )(terms)

    (z,) = call(
        add_kernel, [VMEM] * 2 + [HBM] * 2, [shape(block_shape, bf16)], name="add"
    )(q_own, q_far, terms, agg2)
    (z_pair,) = call(add_kernel, [VMEM] * 2, [shape(block_shape, bf16)], name="add")(z, swap(z, 1))
    z_other = swap(z_pair, 2)
    terms = lax.all_to_all(after(terms, z_pair), ("near", "narrow"), 0, 0)
    out, feats_grad = call(
        finish_kernel,
        [SMEM] + [VMEM] * 8,
        [shape((nodes, hidden), bf16), shape((nodes, width), bf16)],
        name="finish",
    )(place, agg, agg2, agg13, weight, z_pair, z_other, back, inv)
    (weight_grad,) = call(
        weight_grad_kernel, [VMEM, HBM], [shape((width, hidden), f32)], name="weight_grad"
    )(terms, out)
    return (out, feats_grad, weight_grad)


def solution(mesh):
    mesh = Mesh(mesh.devices.reshape(8, 8, 4), ("far", "near", "narrow"))
    rows = P(WIDE, None)
    slots = P(WIDE + ("narrow",))
    placed = (rows, P(WIDE + ("narrow",), None, None), slots, slots, slots, P(), rows)
    return jax.shard_map(
        per_device,
        mesh=mesh,
        in_specs=placed,
        out_specs=(rows, rows, P()),
        check_vma=False,
    )
```
